128 devices in a mesh: role: 2 (over core), dev: 64 (over z, x, y).
Axes of the slice: x: 4, y: 4, z: 4, core: 2. Of those that a mesh axis runs over, the one named last changes fastest.
Arguments:
- queries: bfloat16 [4096, 8192], P(('role', 'dev')), may hold values from -192 to 192, as said below
- key_value_cache: bfloat16 [1024, 256, 1024], P(('role', 'dev')), may hold values from -6 to 6
- guessed_key_value: bfloat16 [4096, 1024], P(('role', 'dev')), may hold values from -6 to 6
- cache_length_per_request: int32 [1024], P(('role', 'dev')), may hold values from 1 to 256, 131072 in all
- moe_rows: bfloat16 [4096, 4096], P(('role', 'dev')), may hold values from -6 to 6
- expert_ids: int32 [4096, 8], P(('role', 'dev')), may hold values from 0 to 127, all different within a row; in each aligned block of 16 rows (0 to 15, 16 to 31, ...) at most 2 rows name the same one
- gate_weights: float32 [4096, 8], P(('role', 'dev')), may hold values from 0.05 to 1
- expert_in: bfloat16 [128, 4096, 1536], P(('role', 'dev')), may hold values from -0.09375 to 0.09375
- expert_down: bfloat16 [128, 768, 4096], P(('role', 'dev')), may hold values from -0.21875 to 0.21875
Outputs:
- attended: bfloat16 [4096, 8192], P(('role', 'dev'))
- moe_out: bfloat16 [4096, 4096], P(('role', 'dev'))
The draws below stay inside these ranges and needn't reach their ends.
Inputs may be any that keep to these rules, and one draw needn't show every extreme that they name: queries of the shown draw lie within -12 and 12. Some request's cache_length_per_request is exactly 256. `expert_ids`: each row names 8 different experts; within each aligned block of 16 rows no expert is named by more than 2 rows, and in every draw some block names some expert exactly 2 times.
All inputs are finite; a program needn't handle non-finite values. No bound on the sum of `cache_length_per_request` on one device may be relied on, other than what follows from the above.
Results may differ from the reference program's by a relative error of at most 0.0058.
Values may be sent and summed in bfloat16 or wider, within the bound.
No kernel may reach another device: no remote copies, remote signals or barrier semaphores. Data moves between devices by JAX's collectives and lax.ppermute only.
A program may use at most 128 MiB of HBM per device.

```python
import math
import jax
import jax.numpy as jnp
import numpy as np
from jax import lax

D = 4096
QUERY_HEADS = 64
KEY_VALUE_HEADS = 4
HEAD_SIZE = 128
TOP = 8
FFW = 768
GUESSED_TOKENS = 4
CONTEXT_SLOTS = 256
EXPERTS = 128
TOK_DEV = 32
HCAP = 2
REQUEST_TOTAL = 1024
TOKEN_TOTAL = 4096
DEVICES = 128


def cache_values(key):
    return jnp.clip(jax.random.normal(key, (REQUEST_TOTAL, CONTEXT_SLOTS, 2 * KEY_VALUE_HEADS * HEAD_SIZE), jnp.float32), -6.0, 6.0)


def draw_key_value_cache(key, part):
    request_offset = cache_values(key)
    return request_offset.astype(jnp.bfloat16)


def draw_queries(key, part):
    key = jax.random.fold_in(key, 2)
    cache_value_rows = jnp.clip(2.0 * jax.random.normal(key, (TOKEN_TOTAL, QUERY_HEADS * HEAD_SIZE), jnp.float32), -12.0, 12.0)
    return cache_value_rows.astype(jnp.bfloat16)


def draw_guessed_key_value(key, part):
    key = jax.random.fold_in(key, 3)
    cache_value_rows = jnp.clip(jax.random.normal(key, (TOKEN_TOTAL, 2 * KEY_VALUE_HEADS * HEAD_SIZE), jnp.float32), -6.0, 6.0)
    return cache_value_rows.astype(jnp.bfloat16)


def levels(stream_key, shape, shards, low, top_value):
    def one(dim, shards_of):
        draws = jax.random.uniform(jax.random.fold_in(jax.random.fold_in(stream_key, 6), dim), (shards_of,), jnp.float32, low / len(shards), top_value / len(shards))
        return jnp.repeat(jnp.exp(draws), shape[dim] // shards_of).reshape((-1,) + (1,) * (len(shape) - dim - 1))

    gain = one(*shards[0])
    for cut in shards[1:]:
        gain = gain * one(*cut)
    return gain


def length_profile(number_of, total, limit, lean):
    loads = [(1 << 20) // math.isqrt(standing ** lean) + 1 for standing in range(2, number_of + 1)]
    spare, given = total - limit - (number_of - 1), [1] * (number_of - 1)
    while spare > 0:
        candidates = [i for i in range(number_of - 1) if given[i] < limit]
        mass, left = sum([loads[i] for i in candidates]), spare
        for i in candidates:
            more = min(limit - given[i], max(1, left * loads[i] // mass), spare)
            given[i] = given[i] + more
            spare = spare - more
    return np.array([limit] + given)


def uneven_parts(key, number_of, total, limit, skew):
    if number_of == 2:
        one = jax.random.randint(key, (), max(1, total - limit), min(limit, total - 1) + 1)
        return jnp.stack([one, total - one])
    tallies = jnp.asarray(length_profile(number_of, total, limit, skew), jnp.int32)
    pairs = (number_of - 1) // 2
    donor, receiver = tallies[1:1 + 2 * pairs:2], tallies[2:2 + 2 * pairs:2]
    slack = jnp.minimum(donor - 1, limit - receiver)
    moved = jax.random.randint(jax.random.fold_in(key, 1), (pairs,), 0, 1 << 20) % (slack + 1)
    tallies = tallies.at[1:1 + 2 * pairs:2].set(donor - moved).at[2:2 + 2 * pairs:2].set(receiver + moved)
    return tallies[jax.random.permutation(jax.random.fold_in(key, 2), number_of)]


def shared_out(stream_key, own, number, rows, amount, top, reach, lean):
    order = jax.random.permutation(stream_key, amount)
    packed, usual = shares(amount, rows * top, reach, lean, True), shares(amount, rows * top, reach, lean, False)
    places = jnp.arange(amount)

    def named(sizes, rotation):
        used = int((sizes > 0).sum())
        fixed = max(1, used // 4)
        shifted = fixed + (places - fixed + rotation * (used - fixed)) % max(1, amount - fixed)
        return jnp.zeros((amount,), jnp.int32).at[order[jnp.where(places < fixed, places, shifted)]].set(jnp.asarray(sizes, jnp.int32))

    sizes = jnp.where(number % 4 == 0, named(packed, number // 4), named(usual, number - number // 4 - 1))
    mixed = jax.random.permutation(jax.random.fold_in(own, 3), amount)
    giver, taker = mixed[0:amount // 2 * 2:2], mixed[1:amount // 2 * 2:2]
    room = jnp.minimum(sizes[giver] - 1, reach - sizes[taker]) // 2
    room = jnp.where((giver == order[0]) | (taker == order[0]) | (sizes[taker] == 0), 0, jnp.maximum(room, 0))
    shifted = jax.random.randint(jax.random.fold_in(own, 4), (amount // 2,), 0, 1 << 20) % (room + 1)
    sizes = sizes.at[giver].add(-shifted).at[taker].add(shifted)
    members = jnp.searchsorted(jnp.cumsum(sizes), jnp.arange(rows * top), side="right").astype(jnp.int32)
    listing = members.reshape(top, rows).T
    listing = listing[jax.random.permutation(jax.random.fold_in(own, 1), rows)]
    rotation = jax.random.randint(jax.random.fold_in(own, 2), (rows, 1), 0, top)
    return jnp.take_along_axis(listing, (jnp.arange(top)[None, :] + rotation) % top, axis=1)


def shares(amount, total, bound, lean, full):
    portions = [(1 << 20) // math.isqrt(grade ** lean) + 1 for grade in range(1, amount + 1)]
    largest = bound if full else min(bound, max(-(-total // amount), total * portions[0] // sum(portions)))
    least = 1 if total - largest >= amount - 1 else 0
    given, rest = [largest] + [least] * (amount - 1), total - largest - least * (amount - 1)
    while rest > 0:
        candidates = [i for i in range(1, amount) if given[i] < largest] or [i for i in range(1, amount) if given[i] < bound]
        whole, remaining = sum([portions[i] for i in candidates]), rest
        for i in candidates:
            more = min(bound - given[i], max(1, remaining * portions[i] // whole), rest)
            given[i] = given[i] + more
            rest = rest - more
    return np.array(given)


def normal_values(own_key, dims, width, limit, split=(), kind=jnp.bfloat16):
    loudness = levels(own_key, dims, split, -0.22, 0.18) if split else 1.0
    entries = jax.random.normal(own_key, dims, jnp.float32) * width * loudness
    return jnp.minimum(jnp.maximum(entries, -limit), limit).astype(kind)


def setup_inputs(seed: int = 0) -> dict:
    seeds = jax.random.split(jax.random.key(seed), 10)
    queries = draw_queries(jax.random.fold_in(seeds[9], 71), 0)
    key_value_cache = draw_key_value_cache(jax.random.fold_in(seeds[9], 71), 0)
    guessed_key_value = draw_guessed_key_value(jax.random.fold_in(seeds[9], 71), 0)
    cache_length_per_request = uneven_parts(seeds[3], REQUEST_TOTAL, REQUEST_TOTAL * CONTEXT_SLOTS // 2, CONTEXT_SLOTS, 1).astype(jnp.int32)
    moe_rows = normal_values(seeds[4], (TOKEN_TOTAL, D), 1.0, 6.0, ((0, 128),))
    expert_ids_keys = jax.random.split(jax.random.fold_in(seeds[5], 1), TOKEN_TOTAL // (TOK_DEV // 2))
    expert_ids_turns = jax.random.permutation(jax.random.fold_in(seeds[5], 3), TOKEN_TOTAL // (TOK_DEV // 2))
    expert_ids = jax.vmap(lambda own, number: shared_out(jax.random.fold_in(seeds[5], 2), own, number, TOK_DEV // 2, EXPERTS, TOP, HCAP, 2))(expert_ids_keys, expert_ids_turns).reshape((TOKEN_TOTAL, TOP))
    gate_weights = jnp.clip(jnp.exp(math.log(1.0) - 2.9957323 * jax.random.uniform(seeds[6], (TOKEN_TOTAL, TOP), jnp.float32) ** levels(seeds[6], (TOKEN_TOTAL, TOP), ((0, 128),), -0.2, 0.2)), 0.05, 1.0)
    expert_in = normal_values(seeds[7], (EXPERTS, D, 2 * FFW), D ** -0.5, 0.09375, ((0, 128),))
    expert_down = normal_values(seeds[8], (EXPERTS, FFW, D), FFW ** -0.5, 0.21875, ((0, 128),))
    return dict(queries=queries, key_value_cache=key_value_cache, guessed_key_value=guessed_key_value, cache_length_per_request=cache_length_per_request, moe_rows=moe_rows, expert_ids=expert_ids, gate_weights=gate_weights, expert_in=expert_in, expert_down=expert_down)


def attend_single_request(items):
    query_rows, request_cache, guessed_rows, length = items
    query_group_size = QUERY_HEADS // KEY_VALUE_HEADS
    feature_width = KEY_VALUE_HEADS * HEAD_SIZE
    scale = float(HEAD_SIZE) ** -0.5
    query_float = query_rows.astype(jnp.float32).reshape(GUESSED_TOKENS, KEY_VALUE_HEADS, query_group_size, HEAD_SIZE)
    cache_key_rows = request_cache[:, :feature_width].astype(jnp.float32).reshape(CONTEXT_SLOTS, KEY_VALUE_HEADS, HEAD_SIZE)
    cache_value_rows = request_cache[:, feature_width:].astype(jnp.float32).reshape(CONTEXT_SLOTS, KEY_VALUE_HEADS, HEAD_SIZE)
    guessed_keys = guessed_rows[:, :feature_width].astype(jnp.float32).reshape(GUESSED_TOKENS, KEY_VALUE_HEADS, HEAD_SIZE)
    guessed_values = guessed_rows[:, feature_width:].astype(jnp.float32).reshape(GUESSED_TOKENS, KEY_VALUE_HEADS, HEAD_SIZE)
    scores_cache = jnp.einsum("sngd,cnd->sngc", query_float, cache_key_rows) * scale
    scores_fresh = jnp.einsum("sngd,jnd->sngj", query_float, guessed_keys) * scale
    valid_cache = (jnp.arange(CONTEXT_SLOTS) < length)[None, None, None, :]
    valid_fresh = (jnp.arange(GUESSED_TOKENS)[None, :] <= jnp.arange(GUESSED_TOKENS)[:, None])[:, None, None, :]
    scores_cache = jnp.where(valid_cache, scores_cache, -jnp.inf)
    scores_fresh = jnp.where(valid_fresh, scores_fresh, -jnp.inf)
    highest = jnp.maximum(jnp.max(scores_cache, axis=-1, keepdims=True), jnp.max(scores_fresh, axis=-1, keepdims=True))
    exp_cache = jnp.exp(scores_cache - highest)
    exp_fresh = jnp.exp(scores_fresh - highest)
    total = jnp.sum(exp_cache, axis=-1, keepdims=True) + jnp.sum(exp_fresh, axis=-1, keepdims=True)
    probs_cache = (exp_cache / total).astype(jnp.bfloat16).astype(jnp.float32)
    probs_fresh = (exp_fresh / total).astype(jnp.bfloat16).astype(jnp.float32)
    output = jnp.einsum("sngc,cnd->sngd", probs_cache, cache_value_rows) + jnp.einsum("sngj,jnd->sngd", probs_fresh, guessed_values)
    return output.reshape(GUESSED_TOKENS, QUERY_HEADS * HEAD_SIZE).astype(jnp.bfloat16)


def reference(queries, key_value_cache, guessed_key_value, cache_length_per_request, moe_rows, expert_ids, gate_weights, expert_in, expert_down):
    attended = lax.map(attend_single_request, (queries.reshape(REQUEST_TOTAL, GUESSED_TOKENS, QUERY_HEADS * HEAD_SIZE), key_value_cache, guessed_key_value.reshape(REQUEST_TOTAL, GUESSED_TOKENS, 2 * KEY_VALUE_HEADS * HEAD_SIZE), cache_length_per_request))
    attended = attended.reshape(TOKEN_TOTAL, QUERY_HEADS * HEAD_SIZE)
    route_weights = gate_weights / jnp.sum(gate_weights, axis=-1, keepdims=True)
    chosen = (expert_ids[:, :, None] == jnp.arange(EXPERTS, dtype=jnp.int32)[None, None, :])
    member_weight = jnp.sum(jnp.where(chosen, route_weights[:, :, None], 0.0), axis=1)
    member = jnp.any(chosen, axis=1).astype(jnp.int32)
    slot_total = DEVICES * 2 * HCAP

    def expert_step(total, expert):
        used = lax.dynamic_index_in_dim(member.T, expert, 0, keepdims=False)
        weight_col = lax.dynamic_index_in_dim(member_weight.T, expert, 0, keepdims=False)
        order = jnp.argsort(1 - used, stable=True)[:slot_total].astype(jnp.int32)
        rows = moe_rows[order]
        joint = jnp.dot(rows, lax.dynamic_index_in_dim(expert_in, expert, 0, keepdims=False), preferred_element_type=jnp.float32)
        hidden = (jax.nn.silu(joint[:, :FFW]) * joint[:, FFW:]).astype(jnp.bfloat16)
        result = jnp.dot(hidden, lax.dynamic_index_in_dim(expert_down, expert, 0, keepdims=False), preferred_element_type=jnp.float32).astype(jnp.bfloat16)
        total = total.at[order].add(weight_col[order][:, None] * result.astype(jnp.float32))
        return total, None

    start = jnp.zeros((TOKEN_TOTAL, D), jnp.float32)
    total, _ = lax.scan(expert_step, start, jnp.arange(EXPERTS, dtype=jnp.int32))
    return attended, total.astype(jnp.bfloat16)
```

```python
import functools

import jax
import jax.numpy as jnp
from jax import lax
from jax.experimental import pallas as pl
from jax.experimental.pallas import tpu as pltpu
from jax.sharding import PartitionSpec as P

QUERY_HEADS = 64
KEY_VALUE_HEADS = 4
HEAD_SIZE = 128
BLOCK_ROWS = 16
BLOCK_SLOTS = 2


def attend(queries, key_value_cache, guessed_key_value, cache_length_per_request):
    request_number, slot_positions, joint_width = key_value_cache.shape
    feature_width = joint_width // 2
    guessed_count = queries.shape[0] // request_number
    query_group_size = QUERY_HEADS // KEY_VALUE_HEADS
    scale = float(HEAD_SIZE) ** (-0.5)
    query_rows = queries.reshape(
        request_number, guessed_count, KEY_VALUE_HEADS, query_group_size, HEAD_SIZE
    )
    cache_key_rows = key_value_cache[:, :, :feature_width].reshape(
        request_number, slot_positions, KEY_VALUE_HEADS, HEAD_SIZE
    )
    cache_value_rows = key_value_cache[:, :, feature_width:].reshape(
        request_number, slot_positions, KEY_VALUE_HEADS, HEAD_SIZE
    )
    guessed_rows = guessed_key_value.reshape(request_number, guessed_count, joint_width)
    guessed_keys = guessed_rows[:, :, :feature_width].reshape(
        request_number, guessed_count, KEY_VALUE_HEADS, HEAD_SIZE
    )
    guessed_values = guessed_rows[:, :, feature_width:].reshape(
        request_number, guessed_count, KEY_VALUE_HEADS, HEAD_SIZE
    )
    scores_cache = (
        jnp.einsum(
            "rsngd,rcnd->rsngc", query_rows, cache_key_rows, preferred_element_type=jnp.float32
        )
        * scale
    )
    scores_fresh = (
        jnp.einsum(
            "rsngd,rjnd->rsngj", query_rows, guessed_keys, preferred_element_type=jnp.float32
        )
        * scale
    )
    valid_cache = (jnp.arange(slot_positions)[None, :] < cache_length_per_request[:, None])[
        :, None, None, None, :
    ]
    valid_fresh = (jnp.arange(guessed_count)[None, :] <= jnp.arange(guessed_count)[:, None])[
        None, :, None, None, :
    ]
    scores_cache = jnp.where(valid_cache, scores_cache, -jnp.inf)
    scores_fresh = jnp.where(valid_fresh, scores_fresh, -jnp.inf)
    highest = jnp.maximum(
        jnp.max(scores_cache, axis=-1, keepdims=True), jnp.max(scores_fresh, axis=-1, keepdims=True)
    )
    exp_cache = jnp.exp(scores_cache - highest)
    exp_fresh = jnp.exp(scores_fresh - highest)
    total = jnp.sum(exp_cache, axis=-1, keepdims=True) + jnp.sum(exp_fresh, axis=-1, keepdims=True)
    probs_cache = (exp_cache / total).astype(jnp.bfloat16)
    probs_fresh = (exp_fresh / total).astype(jnp.bfloat16)
    output = jnp.einsum(
        "rsngc,rcnd->rsngd", probs_cache, cache_value_rows, preferred_element_type=jnp.float32
    )
    output = output + jnp.einsum(
        "rsngj,rjnd->rsngd", probs_fresh, guessed_values, preferred_element_type=jnp.float32
    )
    return output.reshape(request_number * guessed_count, QUERY_HEADS * HEAD_SIZE).astype(
        jnp.bfloat16
    )


def expert_spots(ids, base, chips):
    token_count, top_count = ids.shape
    slots = token_count // BLOCK_ROWS * BLOCK_SLOTS
    shape = (token_count, chips * slots)
    column = lax.broadcasted_iota(jnp.int32, shape, 1)
    expert = base + column // slots
    matches = [ids[:, k : k + 1] == expert for k in range(top_count)]
    member = functools.reduce(jnp.logical_or, matches)
    here = lax.broadcasted_iota(jnp.int32, (token_count, token_count), 0)
    there = lax.broadcasted_iota(jnp.int32, (token_count, token_count), 1)
    earlier = (there < here) & (there // BLOCK_ROWS == here // BLOCK_ROWS)
    ranks = jnp.dot(
        jnp.where(earlier, 1.0, 0.0).astype(jnp.bfloat16),
        jnp.where(member, 1.0, 0.0).astype(jnp.bfloat16),
        preferred_element_type=jnp.float32,
    ).astype(jnp.int32)
    block = lax.broadcasted_iota(jnp.int32, shape, 0) // BLOCK_ROWS
    taken = member & (block * BLOCK_SLOTS + ranks == column % slots)
    return matches, taken


def place_kernel(chips, base_ref, own_ids, other_ids, own_ref, other_ref, out_ref, spots):
    @pl.when(pl.program_id(0) == 0)
    def _():
        ids = jnp.concatenate([own_ids[...], other_ids[...]], axis=0)
        _, taken = expert_spots(ids, base_ref[0], chips)
        spots[...] = jnp.where(taken, 1.0, 0.0).astype(jnp.bfloat16)

    rows = jnp.concatenate([own_ref[...], other_ref[...]], axis=0)
    out_ref[...] = lax.dot_general(
        spots[...], rows, (((0,), (0,)), ((), ())), preferred_element_type=jnp.float32
    ).astype(jnp.bfloat16)


def place(base, own_ids, other_ids, own, other, chips):
    row_count, width = own.shape
    slots = 2 * row_count // BLOCK_ROWS * BLOCK_SLOTS
    tile = min(width, 1024)
    whole = pl.BlockSpec(own_ids.shape, lambda i: (0, 0))
    part = pl.BlockSpec((row_count, tile), lambda i: (0, i))
    return pl.pallas_call(
        functools.partial(place_kernel, chips),
        grid=(width // tile,),
        out_shape=pltpu.HBM((chips * slots, width), jnp.bfloat16),
        in_specs=[pl.BlockSpec(memory_space=pltpu.SMEM), whole, whole, part, part],
        out_specs=pl.BlockSpec((chips * slots, tile), lambda i: (0, i)),
        scratch_shapes=[pltpu.VMEM((2 * row_count, chips * slots), jnp.bfloat16)],
        compiler_params=pltpu.CompilerParams(vmem_limit_bytes=16 << 20),
        name="place_rows",
    )(base, own_ids, other_ids, own, other)


def mix_kernel(
    chips, base_ref, own_ids, other_ids, own_gates, other_gates, in_ref, own_ref, other_ref, spread
):
    row_count = own_ids.shape[0]
    token_count = 2 * row_count

    @pl.when(pl.program_id(0) == 0)
    def _():
        ids = jnp.concatenate([own_ids[...], other_ids[...]], axis=0)
        gates = jnp.concatenate([own_gates[...], other_gates[...]], axis=0)
        matches, taken = expert_spots(ids, base_ref[0], chips)
        route = gates / jnp.sum(gates, axis=-1, keepdims=True)
        weight = sum(
            jnp.where(match, route[:, k : k + 1], 0.0) for k, match in enumerate(matches)
        )
        weight = jnp.where(taken, weight, 0.0)
        high = weight.astype(jnp.bfloat16)
        spread[:token_count] = high
        spread[token_count:] = (weight - high.astype(jnp.float32)).astype(jnp.bfloat16)

    total = jnp.dot(spread[...], in_ref[...], preferred_element_type=jnp.float32)
    total = total[:token_count] + total[token_count:]
    own_ref[...] = total[:row_count]
    other_ref[...] = total[row_count:].astype(jnp.bfloat16)


def mix(base, own_ids, other_ids, own_gates, other_gates, returned, chips):
    row_count = own_ids.shape[0]
    slot_total, width = returned.shape
    tile = min(width, 1024)
    whole = pl.BlockSpec(own_ids.shape, lambda i: (0, 0))
    part = pl.BlockSpec((row_count, tile), lambda i: (0, i))
    return pl.pallas_call(
        functools.partial(mix_kernel, chips),
        grid=(width // tile,),
        out_shape=(
            jax.ShapeDtypeStruct((row_count, width), jnp.float32),
            jax.ShapeDtypeStruct((row_count, width), jnp.bfloat16),
        ),
        in_specs=[
            pl.BlockSpec(memory_space=pltpu.SMEM),
            whole,
            whole,
            whole,
            whole,
            pl.BlockSpec((slot_total, tile), lambda i: (0, i)),
        ],
        out_specs=(part, part),
        scratch_shapes=[pltpu.VMEM((4 * row_count, slot_total), jnp.bfloat16)],
        compiler_params=pltpu.CompilerParams(vmem_limit_bytes=16 << 20),
        name="mix_results",
    )(base, own_ids, other_ids, own_gates, other_gates, returned)


def expert_kernel(rows_hbm, in_ref, down_ref, out_hbm, rows, joint, hidden, out, row_sems, out_sems):
    in_steps, _, depth = rows.shape
    out_steps, _, width = out.shape
    hidden_width = hidden.shape[1]

    def arrive(step):
        return pltpu.make_async_copy(
            rows_hbm.at[:, pl.ds(step * depth, depth)], rows.at[step], row_sems.at[step]
        )

    def leave(step):
        return pltpu.make_async_copy(
            out.at[step], out_hbm.at[:, pl.ds(step * width, width)], out_sems.at[step]
        )

    for step in range(in_steps):
        arrive(step).start()
    for step in range(in_steps):
        arrive(step).wait()
        part = jnp.dot(
            rows[step],
            in_ref[0, step * depth : (step + 1) * depth, :],
            preferred_element_type=jnp.float32,
        )
        joint[...] = part if step == 0 else joint[...] + part
    gate = joint[:, :hidden_width]
    hidden[...] = (gate / (1.0 + jnp.exp(-gate)) * joint[:, hidden_width:]).astype(jnp.bfloat16)
    for step in range(out_steps):
        out[step] = jnp.dot(
            hidden[...],
            down_ref[0, :, step * width : (step + 1) * width],
            preferred_element_type=jnp.float32,
        ).astype(jnp.bfloat16)
        leave(step).start()
    for step in range(out_steps):
        leave(step).wait()


def expert(rows, expert_in, expert_down):
    row_count, width = rows.shape
    hidden_width = expert_down.shape[1]
    depth = min(width, 1024)
    steps = width // depth
    return pl.pallas_call(
        expert_kernel,
        out_shape=pltpu.HBM((row_count, width), jnp.bfloat16),
        in_specs=[
            pl.BlockSpec(memory_space=pl.ANY),
            pl.BlockSpec(memory_space=pltpu.VMEM),
            pl.BlockSpec(memory_space=pltpu.VMEM),
        ],
        out_specs=pl.BlockSpec(memory_space=pl.ANY),
        scratch_shapes=[
            pltpu.VMEM((steps, row_count, depth), jnp.bfloat16),
            pltpu.VMEM((row_count, 2 * hidden_width), jnp.float32),
            pltpu.VMEM((row_count, hidden_width), jnp.bfloat16),
            pltpu.VMEM((steps, row_count, depth), jnp.bfloat16),
            pltpu.SemaphoreType.DMA((steps,)),
            pltpu.SemaphoreType.DMA((steps,)),
        ],
        compiler_params=pltpu.CompilerParams(vmem_limit_bytes=20 << 20),
        cost_estimate=pl.CostEstimate(
            flops=6 * row_count * width * hidden_width,
            bytes_accessed=4 * row_count * width,
            transcendentals=row_count * hidden_width,
        ),
        name="expert_layer",
    )(
        pltpu.with_memory_space_constraint(rows, pltpu.HBM),
        pltpu.with_memory_space_constraint(expert_in, pltpu.VMEM),
        pltpu.with_memory_space_constraint(expert_down, pltpu.VMEM),
    )


def body(
    queries,
    key_value_cache,
    guessed_key_value,
    cache_length_per_request,
    moe_rows,
    expert_ids,
    gate_weights,
    expert_in,
    expert_down,
):
    role = lax.axis_index("role")
    chips = lax.axis_size("dev")
    model_width = moe_rows.shape[1]
    swap = [(0, 1), (1, 0)]
    base = jnp.full((1,), role * chips, jnp.int32)
    other_ids = lax.ppermute(expert_ids, "role", swap)
    other_rows = lax.ppermute(moe_rows, "role", swap)
    other_gates = lax.ppermute(gate_weights, "role", swap)
    outgoing = place(base, expert_ids, other_ids, moe_rows, other_rows, chips)
    arrived = lax.all_to_all(
        outgoing.reshape(chips, -1, model_width), "dev", split_axis=0, concat_axis=0, tiled=True
    )
    result = expert(arrived.reshape(-1, model_width), expert_in, expert_down)
    returned = lax.all_to_all(
        result.reshape(chips, -1, model_width), "dev", split_axis=0, concat_axis=0, tiled=True
    )
    own, other = mix(
        base,
        expert_ids,
        other_ids,
        gate_weights,
        other_gates,
        returned.reshape(-1, model_width),
        chips,
    )
    mixed = (own + lax.ppermute(other, "role", swap).astype(jnp.float32)).astype(jnp.bfloat16)
    attended = attend(queries, key_value_cache, guessed_key_value, cache_length_per_request)
    return (attended, mixed)


def solution(mesh):
    return jax.shard_map(
        body,
        mesh=mesh,
        in_specs=(
            P(("role", "dev"), None),
            P(("role", "dev"), None, None),
            P(("role", "dev"), None),
            P(("role", "dev")),
            P(("role", "dev"), None),
            P(("role", "dev"), None),
            P(("role", "dev"), None),
            P(("role", "dev"), None, None),
            P(("role", "dev"), None, None),
        ),
        out_specs=(P(("role", "dev"), None), P(("role", "dev"), None)),
        check_vma=False,
    )
```

```python
import functools

import jax
import jax.numpy as jnp
from jax import lax
from jax.experimental import pallas as pl
from jax.experimental.pallas import tpu as pltpu
from jax.sharding import PartitionSpec as P

QUERY_HEADS = 64
KEY_VALUE_HEADS = 4
HEAD_SIZE = 128
BLOCK_ROWS = 16
BLOCK_SLOTS = 2
ROW_PARTS = 2
COLUMN_PARTS = 4


def attend(queries, key_value_cache, guessed_key_value, cache_length_per_request):
    request_number, slot_positions, joint_width = key_value_cache.shape
    feature_width = joint_width // 2
    guessed_count = queries.shape[0] // request_number
    query_group_size = QUERY_HEADS // KEY_VALUE_HEADS
    scale = float(HEAD_SIZE) ** (-0.5)
    query_rows = queries.reshape(
        request_number, guessed_count, KEY_VALUE_HEADS, query_group_size, HEAD_SIZE
    )
    cache_key_rows = key_value_cache[:, :, :feature_width].reshape(
        request_number, slot_positions, KEY_VALUE_HEADS, HEAD_SIZE
    )
    cache_value_rows = key_value_cache[:, :, feature_width:].reshape(
        request_number, slot_positions, KEY_VALUE_HEADS, HEAD_SIZE
    )
    guessed_rows = guessed_key_value.reshape(request_number, guessed_count, joint_width)
    guessed_keys = guessed_rows[:, :, :feature_width].reshape(
        request_number, guessed_count, KEY_VALUE_HEADS, HEAD_SIZE
    )
    guessed_values = guessed_rows[:, :, feature_width:].reshape(
        request_number, guessed_count, KEY_VALUE_HEADS, HEAD_SIZE
    )
    scores_cache = (
        jnp.einsum(
            "rsngd,rcnd->rsngc", query_rows, cache_key_rows, preferred_element_type=jnp.float32
        )
        * scale
    )
    scores_fresh = (
        jnp.einsum(
            "rsngd,rjnd->rsngj", query_rows, guessed_keys, preferred_element_type=jnp.float32
        )
        * scale
    )
    valid_cache = (jnp.arange(slot_positions)[None, :] < cache_length_per_request[:, None])[
        :, None, None, None, :
    ]
    valid_fresh = (jnp.arange(guessed_count)[None, :] <= jnp.arange(guessed_count)[:, None])[
        None, :, None, None, :
    ]
    scores_cache = jnp.where(valid_cache, scores_cache, -jnp.inf)
    scores_fresh = jnp.where(valid_fresh, scores_fresh, -jnp.inf)
    highest = jnp.maximum(
        jnp.max(scores_cache, axis=-1, keepdims=True), jnp.max(scores_fresh, axis=-1, keepdims=True)
    )
    exp_cache = jnp.exp(scores_cache - highest)
    exp_fresh = jnp.exp(scores_fresh - highest)
    total = jnp.sum(exp_cache, axis=-1, keepdims=True) + jnp.sum(exp_fresh, axis=-1, keepdims=True)
    probs_cache = (exp_cache / total).astype(jnp.bfloat16)
    probs_fresh = (exp_fresh / total).astype(jnp.bfloat16)
    output = jnp.einsum(
        "rsngc,rcnd->rsngd", probs_cache, cache_value_rows, preferred_element_type=jnp.float32
    )
    output = output + jnp.einsum(
        "rsngj,rjnd->rsngd", probs_fresh, guessed_values, preferred_element_type=jnp.float32
    )
    return output.reshape(request_number * guessed_count, QUERY_HEADS * HEAD_SIZE).astype(
        jnp.bfloat16
    )


def expert_spots(own_ids, other_ids, base, chips):
    ids = jnp.concatenate([own_ids, other_ids], axis=1)
    top_count, columns = ids.shape
    slots = columns // BLOCK_ROWS * BLOCK_SLOTS
    shape = (chips * slots, columns)
    line = lax.broadcasted_iota(jnp.int32, shape, 0)
    column = lax.broadcasted_iota(jnp.int32, shape, 1)
    serving = base + line // slots
    matches = [ids[k : k + 1, :] == serving for k in range(top_count)]
    member = functools.reduce(jnp.logical_or, matches)
    here = lax.broadcasted_iota(jnp.int32, (columns, columns), 0)
    there = lax.broadcasted_iota(jnp.int32, (columns, columns), 1)
    earlier = (here < there) & (here // BLOCK_ROWS == there // BLOCK_ROWS)
    ranks = jnp.dot(
        jnp.where(member, 1.0, 0.0).astype(jnp.bfloat16),
        jnp.where(earlier, 1.0, 0.0).astype(jnp.bfloat16),
        preferred_element_type=jnp.float32,
    ).astype(jnp.int32)
    return matches, member & (column // BLOCK_ROWS * BLOCK_SLOTS + ranks == line % slots)


def place_kernel(chips, base_ref, own_ids, other_ids, own_ref, other_ref, out_ref, spots):
    @pl.when(pl.program_id(0) == 0)
    def _():
        _, taken = expert_spots(own_ids[...], other_ids[...], base_ref[0], chips)
        spots[...] = jnp.where(taken, 1.0, 0.0).astype(jnp.bfloat16)

    rows = jnp.concatenate([own_ref[...], other_ref[...]], axis=0)
    out_ref[...] = jnp.dot(spots[...], rows, preferred_element_type=jnp.float32).astype(
        jnp.bfloat16
    )


def place(base, own_ids, other_ids, own, other, chips):
    row_count, width = own.shape
    lines = chips * 2 * row_count // BLOCK_ROWS * BLOCK_SLOTS
    tile = min(width, 1024)
    whole = pl.BlockSpec(own_ids.shape, lambda i: (0, 0))
    part = pl.BlockSpec((row_count, tile), lambda i: (0, i))
    return pl.pallas_call(
        functools.partial(place_kernel, chips),
        grid=(width // tile,),
        out_shape=jax.ShapeDtypeStruct((lines, width), jnp.bfloat16),
        in_specs=[pl.BlockSpec(memory_space=pltpu.SMEM), whole, whole, part, part],
        out_specs=pl.BlockSpec((lines, tile), lambda i: (0, i)),
        scratch_shapes=[pltpu.VMEM((lines, 2 * row_count), jnp.bfloat16)],
        compiler_params=pltpu.CompilerParams(vmem_limit_bytes=12 << 20),
        name="place_rows",
    )(base, own_ids, other_ids, own, other)


def weigh_kernel(chips, base_ref, own_ids, other_ids, own_gates, other_gates, out_ref):
    columns = out_ref.shape[0] // 2
    matches, taken = expert_spots(own_ids[...], other_ids[...], base_ref[0], chips)
    gates = jnp.concatenate([own_gates[...], other_gates[...]], axis=1)
    route = gates / jnp.sum(gates, axis=0, keepdims=True)
    weight = sum(jnp.where(match, route[k : k + 1, :], 0.0) for k, match in enumerate(matches))
    weight = jnp.where(taken, weight, 0.0).T
    high = weight.astype(jnp.bfloat16)
    out_ref[:columns] = high
    out_ref[columns:] = (weight - high.astype(jnp.float32)).astype(jnp.bfloat16)


def weigh(base, own_ids, other_ids, own_gates, other_gates, lines):
    vmem = pl.BlockSpec(memory_space=pltpu.VMEM)
    chips = lines * BLOCK_ROWS // (2 * own_ids.shape[1] * BLOCK_SLOTS)
    return pl.pallas_call(
        functools.partial(weigh_kernel, chips),
        out_shape=jax.ShapeDtypeStruct((4 * own_ids.shape[1], lines), jnp.bfloat16),
        in_specs=[pl.BlockSpec(memory_space=pltpu.SMEM)] + [vmem] * 4,
        out_specs=vmem,
        compiler_params=pltpu.CompilerParams(vmem_limit_bytes=12 << 20),
        name="weigh_lines",
    )(base, own_ids, other_ids, own_gates, other_gates)


def mix_kernel(spread, in_ref, own_ref, other_ref):
    row_count = own_ref.shape[0]
    total = jnp.dot(spread[...], in_ref[...], preferred_element_type=jnp.float32)
    total = total[: 2 * row_count] + total[2 * row_count :]
    own_ref[...] = total[:row_count]
    other_ref[...] = total[row_count:].astype(jnp.bfloat16)


def mix(spread, returned):
    row_count = spread.shape[0] // 4
    lines, width = returned.shape
    tile = min(width, 1024)
    part = pl.BlockSpec((row_count, tile), lambda i: (0, i))
    return pl.pallas_call(
        mix_kernel,
        grid=(width // tile,),
        out_shape=(
            jax.ShapeDtypeStruct((row_count, width), jnp.float32),
            jax.ShapeDtypeStruct((row_count, width), jnp.bfloat16),
        ),
        in_specs=[
            pl.BlockSpec(spread.shape, lambda i: (0, 0)),
            pl.BlockSpec((lines, tile), lambda i: (0, i)),
        ],
        out_specs=(part, part),
        compiler_params=pltpu.CompilerParams(vmem_limit_bytes=12 << 20),
        name="mix_results",
    )(spread, returned)


def expert_kernel(rows, in_ref, down_hbm, out_hbm, down, joint, hidden, out, down_sem, out_sems):
    row_count, width = rows.shape
    hidden_width = hidden.shape[1]
    block = row_count // ROW_PARTS
    cut = width // COLUMN_PARTS

    def leave(part, step):
        place = (pl.ds(part * block, block), pl.ds(step * cut, cut))
        return pltpu.make_async_copy(out.at[place], out_hbm.at[place], out_sems.at[part, step])

    fetch = pltpu.make_async_copy(down_hbm, down, down_sem.at[0])
    fetch.start()
    for part in range(ROW_PARTS):
        lines = slice(part * block, (part + 1) * block)
        joint[lines] = jnp.dot(rows[lines], in_ref[0], preferred_element_type=jnp.float32)
        gate = joint[lines, :hidden_width]
        hidden[lines] = (gate / (1.0 + jnp.exp(-gate)) * joint[lines, hidden_width:]).astype(
            jnp.bfloat16
        )
        if part == 0:
            fetch.wait()
        for step in range(COLUMN_PARTS):
            columns = slice(step * cut, (step + 1) * cut)
            out[lines, columns] = jnp.dot(
                hidden[lines], down[0, :, columns], preferred_element_type=jnp.float32
            ).astype(jnp.bfloat16)
            leave(part, step).start()
    for part in range(ROW_PARTS):
        for step in range(COLUMN_PARTS):
            leave(part, step).wait()


def expert(rows, expert_in, expert_down):
    row_count, width = rows.shape
    hidden_width = expert_down.shape[1]
    return pl.pallas_call(
        expert_kernel,
        out_shape=pltpu.HBM((row_count, width), jnp.bfloat16),
        in_specs=[
            pl.BlockSpec(memory_space=pltpu.VMEM),
            pl.BlockSpec(memory_space=pltpu.VMEM),
            pl.BlockSpec(memory_space=pl.ANY),
        ],
        out_specs=pl.BlockSpec(memory_space=pl.ANY),
        scratch_shapes=[
            pltpu.VMEM(expert_down.shape, jnp.bfloat16),
            pltpu.VMEM((row_count, 2 * hidden_width), jnp.float32),
            pltpu.VMEM((row_count, hidden_width), jnp.bfloat16),
            pltpu.VMEM((row_count, width), jnp.bfloat16),
            pltpu.SemaphoreType.DMA((1,)),
            pltpu.SemaphoreType.DMA((ROW_PARTS, COLUMN_PARTS)),
        ],
        compiler_params=pltpu.CompilerParams(vmem_limit_bytes=24 << 20),
        cost_estimate=pl.CostEstimate(
            flops=6 * row_count * width * hidden_width,
            bytes_accessed=4 * row_count * width,
            transcendentals=row_count * hidden_width,
        ),
        name="expert_layer",
    )(
        pltpu.with_memory_space_constraint(rows, pltpu.VMEM),
        pltpu.with_memory_space_constraint(expert_in, pltpu.VMEM),
        pltpu.with_memory_space_constraint(expert_down, pltpu.HBM),
    )


def body(
    queries,
    key_value_cache,
    guessed_key_value,
    cache_length_per_request,
    moe_rows,
    expert_ids,
    gate_weights,
    expert_in,
    expert_down,
):
    role = lax.axis_index("role")
    chips = lax.axis_size("dev")
    model_width = moe_rows.shape[1]
    swap = [(0, 1), (1, 0)]
    base = jnp.full((1,), role * chips, jnp.int32)

    def exchange(lines):
        blocks = lines.reshape(chips, -1, model_width)
        moved = lax.all_to_all(blocks, "dev", split_axis=0, concat_axis=0, tiled=True)
        return moved.reshape(-1, model_width)

    ids = expert_ids.T
    other_ids = lax.ppermute(ids, "role", swap)
    other_rows = lax.ppermute(moe_rows, "role", swap)
    outgoing = place(base, ids, other_ids, moe_rows, other_rows, chips)
    outgoing, expert_in = lax.optimization_barrier((outgoing, expert_in))
    result = expert(exchange(outgoing), expert_in, expert_down)
    result, gates = lax.optimization_barrier((result, gate_weights.T))
    other_gates = lax.ppermute(gates, "role", swap)
    spread = weigh(base, ids, other_ids, gates, other_gates, result.shape[0])
    own, other = mix(spread, exchange(result))
    mixed = (own + lax.ppermute(other, "role", swap).astype(jnp.float32)).astype(jnp.bfloat16)
    attended = attend(queries, key_value_cache, guessed_key_value, cache_length_per_request)
    return (attended, mixed)


def solution(mesh):
    return jax.shard_map(
        body,
        mesh=mesh,
        in_specs=(
            P(("role", "dev"), None),
            P(("role", "dev"), None, None),
            P(("role", "dev"), None),
            P(("role", "dev")),
            P(("role", "dev"), None),
            P(("role", "dev"), None),
            P(("role", "dev"), None),
            P(("role", "dev"), None, None),
            P(("role", "dev"), None, None),
        ),
        out_specs=(P(("role", "dev"), None), P(("role", "dev"), None)),
        check_vma=False,
    )
```

```python
import functools

import jax
import jax.numpy as jnp
from jax import lax
from jax.experimental import pallas as pl
from jax.experimental.pallas import tpu as pltpu
from jax.sharding import PartitionSpec as P

QUERY_HEADS = 64
KEY_VALUE_HEADS = 4
HEAD_SIZE = 128
BLOCK_ROWS = 16
BLOCK_SLOTS = 2
ROW_PARTS = 2
COLUMN_PARTS = 4
MIX_PARTS = 8


def attend(queries, key_value_cache, guessed_key_value, cache_length_per_request):
    request_number, slot_positions, joint_width = key_value_cache.shape
    feature_width = joint_width // 2
    guessed_count = queries.shape[0] // request_number
    query_group_size = QUERY_HEADS // KEY_VALUE_HEADS
    scale = float(HEAD_SIZE) ** (-0.5)
    query_rows = queries.reshape(
        request_number, guessed_count, KEY_VALUE_HEADS, query_group_size, HEAD_SIZE
    )
    cache_key_rows = key_value_cache[:, :, :feature_width].reshape(
        request_number, slot_positions, KEY_VALUE_HEADS, HEAD_SIZE
    )
    cache_value_rows = key_value_cache[:, :, feature_width:].reshape(
        request_number, slot_positions, KEY_VALUE_HEADS, HEAD_SIZE
    )
    guessed_rows = guessed_key_value.reshape(request_number, guessed_count, joint_width)
    guessed_keys = guessed_rows[:, :, :feature_width].reshape(
        request_number, guessed_count, KEY_VALUE_HEADS, HEAD_SIZE
    )
    guessed_values = guessed_rows[:, :, feature_width:].reshape(
        request_number, guessed_count, KEY_VALUE_HEADS, HEAD_SIZE
    )
    scores_cache = (
        jnp.einsum(
            "rsngd,rcnd->rsngc", query_rows, cache_key_rows, preferred_element_type=jnp.float32
        )
        * scale
    )
    scores_fresh = (
        jnp.einsum(
            "rsngd,rjnd->rsngj", query_rows, guessed_keys, preferred_element_type=jnp.float32
        )
        * scale
    )
    valid_cache = (jnp.arange(slot_positions)[None, :] < cache_length_per_request[:, None])[
        :, None, None, None, :
    ]
    valid_fresh = (jnp.arange(guessed_count)[None, :] <= jnp.arange(guessed_count)[:, None])[
        None, :, None, None, :
    ]
    scores_cache = jnp.where(valid_cache, scores_cache, -jnp.inf)
    scores_fresh = jnp.where(valid_fresh, scores_fresh, -jnp.inf)
    highest = jnp.maximum(
        jnp.max(scores_cache, axis=-1, keepdims=True), jnp.max(scores_fresh, axis=-1, keepdims=True)
    )
    exp_cache = jnp.exp(scores_cache - highest)
    exp_fresh = jnp.exp(scores_fresh - highest)
    total = jnp.sum(exp_cache, axis=-1, keepdims=True) + jnp.sum(exp_fresh, axis=-1, keepdims=True)
    probs_cache = (exp_cache / total).astype(jnp.bfloat16)
    probs_fresh = (exp_fresh / total).astype(jnp.bfloat16)
    output = jnp.einsum(
        "rsngc,rcnd->rsngd", probs_cache, cache_value_rows, preferred_element_type=jnp.float32
    )
    output = output + jnp.einsum(
        "rsngj,rjnd->rsngd", probs_fresh, guessed_values, preferred_element_type=jnp.float32
    )
    return output.reshape(request_number * guessed_count, QUERY_HEADS * HEAD_SIZE).astype(
        jnp.bfloat16
    )


def expert_spots(own_ids, other_ids, base, chips):
    ids = jnp.concatenate([own_ids, other_ids], axis=1)
    top_count, columns = ids.shape
    slots = columns // BLOCK_ROWS * BLOCK_SLOTS
    shape = (chips * slots, columns)
    line = lax.broadcasted_iota(jnp.int32, shape, 0)
    column = lax.broadcasted_iota(jnp.int32, shape, 1)
    serving = base + line // slots
    matches = [ids[k : k + 1, :] == serving for k in range(top_count)]
    member = functools.reduce(jnp.logical_or, matches)
    here = lax.broadcasted_iota(jnp.int32, (columns, columns), 0)
    there = lax.broadcasted_iota(jnp.int32, (columns, columns), 1)
    earlier = (here < there) & (here // BLOCK_ROWS == there // BLOCK_ROWS)
    ranks = jnp.dot(
        jnp.where(member, 1.0, 0.0).astype(jnp.bfloat16),
        jnp.where(earlier, 1.0, 0.0).astype(jnp.bfloat16),
        preferred_element_type=jnp.float32,
    ).astype(jnp.int32)
    return matches, member & (column // BLOCK_ROWS * BLOCK_SLOTS + ranks == line % slots)


def place_kernel(chips, base_ref, own_ids, other_ids, own_hbm, other_ref, out_ref, rows, row_sem):
    row_count, width = own_hbm.shape
    fetch = pltpu.make_async_copy(own_hbm, rows, row_sem.at[0])
    fetch.start()
    _, taken = expert_spots(own_ids[...], other_ids[...], base_ref[0], chips)
    spots = jnp.where(taken, 1.0, 0.0).astype(jnp.bfloat16)
    fetch.wait()
    cut = width // COLUMN_PARTS
    for step in range(COLUMN_PARTS):
        columns = slice(step * cut, (step + 1) * cut)
        both = jnp.concatenate([rows[:, columns], other_ref[:, columns]], axis=0)
        out_ref[:, columns] = jnp.dot(spots, both, preferred_element_type=jnp.float32).astype(
            jnp.bfloat16
        )


def place(base, own_ids, other_ids, own, other, chips):
    row_count, width = own.shape
    lines = chips * 2 * row_count // BLOCK_ROWS * BLOCK_SLOTS
    vmem = pl.BlockSpec(memory_space=pltpu.VMEM)
    return pl.pallas_call(
        functools.partial(place_kernel, chips),
        out_shape=pltpu.VMEM((lines, width), jnp.bfloat16),
        in_specs=[
            pl.BlockSpec(memory_space=pltpu.SMEM),
            vmem,
            vmem,
            pl.BlockSpec(memory_space=pl.ANY),
            vmem,
        ],
        out_specs=vmem,
        scratch_shapes=[
            pltpu.VMEM((row_count, width), jnp.bfloat16),
            pltpu.SemaphoreType.DMA((1,)),
        ],
        compiler_params=pltpu.CompilerParams(vmem_limit_bytes=12 << 20),
        name="place_rows",
    )(
        base,
        own_ids,
        other_ids,
        pltpu.with_memory_space_constraint(own, pltpu.HBM),
        pltpu.with_memory_space_constraint(other, pltpu.VMEM),
    )


def weigh_kernel(chips, base_ref, own_ids, other_ids, own_gates, other_gates, out_ref):
    columns = out_ref.shape[0] // 2
    matches, taken = expert_spots(own_ids[...], other_ids[...], base_ref[0], chips)
    gates = jnp.concatenate([own_gates[...], other_gates[...]], axis=1)
    route = gates / jnp.sum(gates, axis=0, keepdims=True)
    weight = sum(jnp.where(match, route[k : k + 1, :], 0.0) for k, match in enumerate(matches))
    weight = jnp.where(taken, weight, 0.0).T
    high = weight.astype(jnp.bfloat16)
    out_ref[:columns] = high
    out_ref[columns:] = (weight - high.astype(jnp.float32)).astype(jnp.bfloat16)


def weigh(base, own_ids, other_ids, own_gates, other_gates, lines):
    vmem = pl.BlockSpec(memory_space=pltpu.VMEM)
    chips = lines * BLOCK_ROWS // (2 * own_ids.shape[1] * BLOCK_SLOTS)
    return pl.pallas_call(
        functools.partial(weigh_kernel, chips),
        out_shape=jax.ShapeDtypeStruct((4 * own_ids.shape[1], lines), jnp.bfloat16),
        in_specs=[pl.BlockSpec(memory_space=pltpu.SMEM)] + [vmem] * 4,
        out_specs=vmem,
        compiler_params=pltpu.CompilerParams(vmem_limit_bytes=12 << 20),
        name="weigh_lines",
    )(base, own_ids, other_ids, own_gates, other_gates)


def mix_kernel(spread, in_hbm, own_ref, other_ref, lines, line_sems):
    row_count, width = own_ref.shape
    cut = width // MIX_PARTS

    def arrive(step):
        columns = pl.ds(step * cut, cut)
        return pltpu.make_async_copy(in_hbm.at[:, columns], lines.at[step], line_sems.at[step])

    for step in range(MIX_PARTS):
        arrive(step).start()
    for step in range(MIX_PARTS):
        arrive(step).wait()
        columns = slice(step * cut, (step + 1) * cut)
        total = jnp.dot(spread[...], lines[step], preferred_element_type=jnp.float32)
        total = total[: 2 * row_count] + total[2 * row_count :]
        own_ref[:, columns] = total[:row_count]
        other_ref[:, columns] = total[row_count:].astype(jnp.bfloat16)


def mix(spread, returned):
    row_count = spread.shape[0] // 4
    lines, width = returned.shape
    vmem = pl.BlockSpec(memory_space=pltpu.VMEM)
    return pl.pallas_call(
        mix_kernel,
        out_shape=(
            jax.ShapeDtypeStruct((row_count, width), jnp.float32),
            jax.ShapeDtypeStruct((row_count, width), jnp.bfloat16),
        ),
        in_specs=[vmem, pl.BlockSpec(memory_space=pl.ANY)],
        out_specs=(vmem, vmem),
        scratch_shapes=[
            pltpu.VMEM((MIX_PARTS, lines, width // MIX_PARTS), jnp.bfloat16),
            pltpu.SemaphoreType.DMA((MIX_PARTS,)),
        ],
        compiler_params=pltpu.CompilerParams(vmem_limit_bytes=12 << 20),
        name="mix_results",
    )(spread, pltpu.with_memory_space_constraint(returned, pltpu.HBM))


def expert_kernel(rows, in_ref, down_hbm, out_hbm, down, joint, hidden, out, down_sem, out_sems):
    row_count, width = rows.shape
    hidden_width = hidden.shape[1]
    block = row_count // ROW_PARTS
    cut = width // COLUMN_PARTS

    def leave(part, step):
        place = (pl.ds(part * block, block), pl.ds(step * cut, cut))
        return pltpu.make_async_copy(out.at[place], out_hbm.at[place], out_sems.at[part, step])

    fetch = pltpu.make_async_copy(down_hbm, down, down_sem.at[0])
    fetch.start()
    for part in range(ROW_PARTS):
        lines = slice(part * block, (part + 1) * block)
        joint[lines] = jnp.dot(rows[lines], in_ref[0], preferred_element_type=jnp.float32)
        gate = joint[lines, :hidden_width]
        hidden[lines] = (gate / (1.0 + jnp.exp(-gate)) * joint[lines, hidden_width:]).astype(
            jnp.bfloat16
        )
        if part == 0:
            fetch.wait()
        for step in range(COLUMN_PARTS):
            columns = slice(step * cut, (step + 1) * cut)
            out[lines, columns] = jnp.dot(
                hidden[lines], down[0, :, columns], preferred_element_type=jnp.float32
            ).astype(jnp.bfloat16)
            leave(part, step).start()
    for part in range(ROW_PARTS):
        for step in range(COLUMN_PARTS):
            leave(part, step).wait()


def expert(rows, expert_in, expert_down):
    row_count, width = rows.shape
    hidden_width = expert_down.shape[1]
    return pl.pallas_call(
        expert_kernel,
        out_shape=pltpu.HBM((row_count, width), jnp.bfloat16),
        in_specs=[
            pl.BlockSpec(memory_space=pltpu.VMEM),
            pl.BlockSpec(memory_space=pltpu.VMEM),
            pl.BlockSpec(memory_space=pl.ANY),
        ],
        out_specs=pl.BlockSpec(memory_space=pl.ANY),
        scratch_shapes=[
            pltpu.VMEM(expert_down.shape, jnp.bfloat16),
            pltpu.VMEM((row_count, 2 * hidden_width), jnp.float32),
            pltpu.VMEM((row_count, hidden_width), jnp.bfloat16),
            pltpu.VMEM((row_count, width), jnp.bfloat16),
            pltpu.SemaphoreType.DMA((1,)),
            pltpu.SemaphoreType.DMA((ROW_PARTS, COLUMN_PARTS)),
        ],
        compiler_params=pltpu.CompilerParams(vmem_limit_bytes=24 << 20),
        cost_estimate=pl.CostEstimate(
            flops=6 * row_count * width * hidden_width,
            bytes_accessed=4 * row_count * width,
            transcendentals=row_count * hidden_width,
        ),
        name="expert_layer",
    )(
        pltpu.with_memory_space_constraint(rows, pltpu.VMEM),
        pltpu.with_memory_space_constraint(expert_in, pltpu.VMEM),
        pltpu.with_memory_space_constraint(expert_down, pltpu.HBM),
    )


def body(
    queries,
    key_value_cache,
    guessed_key_value,
    cache_length_per_request,
    moe_rows,
    expert_ids,
    gate_weights,
    expert_in,
    expert_down,
):
    role = lax.axis_index("role")
    chips = lax.axis_size("dev")
    model_width = moe_rows.shape[1]
    swap = [(0, 1), (1, 0)]
    base = jnp.full((1,), role * chips, jnp.int32)

    def exchange(lines):
        blocks = lines.reshape(chips, -1, model_width)
        moved = lax.all_to_all(blocks, "dev", split_axis=0, concat_axis=0, tiled=True)
        return moved.reshape(-1, model_width)

    ids, gates = expert_ids.T, gate_weights.T
    other_ids = lax.ppermute(ids, "role", swap)
    other_rows = lax.ppermute(moe_rows, "role", swap)
    other_gates = lax.ppermute(gates, "role", swap)
    asked = (queries, key_value_cache, guessed_key_value, cache_length_per_request)
    attended = lax.cond(role == 1, attend, lambda queries, *_: jnp.zeros_like(queries), *asked)
    other_rows, other_gates, attended = lax.optimization_barrier(
        (other_rows, other_gates, attended)
    )
    outgoing = place(base, ids, other_ids, moe_rows, other_rows, chips)
    outgoing, expert_in = lax.optimization_barrier((outgoing, expert_in))
    result = expert(exchange(outgoing), expert_in, expert_down)
    result, queries = lax.optimization_barrier((result, queries))
    returned = exchange(result)
    spread = weigh(base, ids, other_ids, gates, other_gates, result.shape[0])
    attended = lax.cond(
        role == 0,
        lambda done, *asked: attend(*asked),
        lambda done, *_: done,
        attended,
        queries,
        *asked[1:],
    )
    returned, spread, attended = lax.optimization_barrier((returned, spread, attended))
    own, other = mix(spread, returned)
    received = lax.ppermute(other, "role", swap)
    mixed = (own + received.astype(jnp.float32)).astype(jnp.bfloat16)
    return (attended, mixed)


def solution(mesh):
    return jax.shard_map(
        body,
        mesh=mesh,
        in_specs=(
            P(("role", "dev"), None),
            P(("role", "dev"), None, None),
            P(("role", "dev"), None),
            P(("role", "dev")),
            P(("role", "dev"), None),
            P(("role", "dev"), None),
            P(("role", "dev"), None),
            P(("role", "dev"), None, None),
            P(("role", "dev"), None, None),
        ),
        out_specs=(P(("role", "dev"), None), P(("role", "dev"), None)),
        check_vma=False,
    )
```

```python
import functools

import jax
import jax.numpy as jnp
from jax import lax
from jax.experimental import pallas as pl
from jax.experimental.pallas import tpu as pltpu
from jax.sharding import PartitionSpec as P

QUERY_HEADS = 64
KEY_VALUE_HEADS = 4
HEAD_SIZE = 128
BLOCK_ROWS = 16
BLOCK_SLOTS = 2
ROW_PARTS = 2
COLUMN_PARTS = 4
MIX_PARTS = 4
ATTEND_CUTS = (2, 4)


def attend(queries, key_value_cache, guessed_key_value, cache_length_per_request):
    request_number, slot_positions, joint_width = key_value_cache.shape
    feature_width = joint_width // 2
    guessed_count = queries.shape[0] // request_number
    query_group_size = QUERY_HEADS // KEY_VALUE_HEADS
    scale = float(HEAD_SIZE) ** (-0.5)
    query_rows = queries.reshape(
        request_number, guessed_count, KEY_VALUE_HEADS, query_group_size, HEAD_SIZE
    )
    cache_key_rows = key_value_cache[:, :, :feature_width].reshape(
        request_number, slot_positions, KEY_VALUE_HEADS, HEAD_SIZE
    )
    cache_value_rows = key_value_cache[:, :, feature_width:].reshape(
        request_number, slot_positions, KEY_VALUE_HEADS, HEAD_SIZE
    )
    guessed_rows = guessed_key_value.reshape(request_number, guessed_count, joint_width)
    guessed_keys = guessed_rows[:, :, :feature_width].reshape(
        request_number, guessed_count, KEY_VALUE_HEADS, HEAD_SIZE
    )
    guessed_values = guessed_rows[:, :, feature_width:].reshape(
        request_number, guessed_count, KEY_VALUE_HEADS, HEAD_SIZE
    )
    scores_cache = (
        jnp.einsum(
            "rsngd,rcnd->rsngc", query_rows, cache_key_rows, preferred_element_type=jnp.float32
        )
        * scale
    )
    scores_fresh = (
        jnp.einsum(
            "rsngd,rjnd->rsngj", query_rows, guessed_keys, preferred_element_type=jnp.float32
        )
        * scale
    )
    valid_cache = (jnp.arange(slot_positions)[None, :] < cache_length_per_request[:, None])[
        :, None, None, None, :
    ]
    valid_fresh = (jnp.arange(guessed_count)[None, :] <= jnp.arange(guessed_count)[:, None])[
        None, :, None, None, :
    ]
    scores_cache = jnp.where(valid_cache, scores_cache, -jnp.inf)
    scores_fresh = jnp.where(valid_fresh, scores_fresh, -jnp.inf)
    highest = jnp.maximum(
        jnp.max(scores_cache, axis=-1, keepdims=True), jnp.max(scores_fresh, axis=-1, keepdims=True)
    )
    exp_cache = jnp.exp(scores_cache - highest)
    exp_fresh = jnp.exp(scores_fresh - highest)
    total = jnp.sum(exp_cache, axis=-1, keepdims=True) + jnp.sum(exp_fresh, axis=-1, keepdims=True)
    probs_cache = (exp_cache / total).astype(jnp.bfloat16)
    probs_fresh = (exp_fresh / total).astype(jnp.bfloat16)
    output = jnp.einsum(
        "rsngc,rcnd->rsngd", probs_cache, cache_value_rows, preferred_element_type=jnp.float32
    )
    output = output + jnp.einsum(
        "rsngj,rjnd->rsngd", probs_fresh, guessed_values, preferred_element_type=jnp.float32
    )
    return output.reshape(request_number * guessed_count, QUERY_HEADS * HEAD_SIZE).astype(
        jnp.bfloat16
    )


def attend_in_groups(queries, key_value_cache, guessed_key_value, cache_length_per_request):
    arrays = (queries, key_value_cache, guessed_key_value, cache_length_per_request)
    requests = key_value_cache.shape[0]
    groups = zip(
        *(
            jnp.split(array, [cut * array.shape[0] // requests for cut in ATTEND_CUTS])
            for array in arrays
        )
    )
    done = []
    for group in groups:
        if done:
            done[-1], group = lax.optimization_barrier((done[-1], group))
        done.append(attend(*group))
    return jnp.concatenate(done)


def expert_spots(own_ids, other_ids, base, chips):
    ids = jnp.concatenate([own_ids, other_ids], axis=1)
    top_count, columns = ids.shape
    slots = columns // BLOCK_ROWS * BLOCK_SLOTS
    shape = (chips * slots, columns)
    line = lax.broadcasted_iota(jnp.int32, shape, 0)
    column = lax.broadcasted_iota(jnp.int32, shape, 1)
    serving = base + line // slots
    matches = [ids[k : k + 1, :] == serving for k in range(top_count)]
    member = functools.reduce(jnp.logical_or, matches)
    here = lax.broadcasted_iota(jnp.int32, (columns, columns), 0)
    there = lax.broadcasted_iota(jnp.int32, (columns, columns), 1)
    earlier = (here < there) & (here // BLOCK_ROWS == there // BLOCK_ROWS)
    ranks = jnp.dot(
        jnp.where(member, 1.0, 0.0).astype(jnp.bfloat16),
        jnp.where(earlier, 1.0, 0.0).astype(jnp.bfloat16),
        preferred_element_type=jnp.float32,
    ).astype(jnp.int32)
    return matches, member & (column // BLOCK_ROWS * BLOCK_SLOTS + ranks == line % slots)


def place_kernel(chips, base_ref, own_ids, other_ids, own_hbm, other_ref, out_ref, rows, row_sem):
    row_count, width = own_hbm.shape
    fetch = pltpu.make_async_copy(own_hbm, rows, row_sem.at[0])
    fetch.start()
    _, taken = expert_spots(own_ids[...], other_ids[...], base_ref[0], chips)
    spots = jnp.where(taken, 1.0, 0.0).astype(jnp.bfloat16)
    fetch.wait()
    cut = width // COLUMN_PARTS
    for step in range(COLUMN_PARTS):
        columns = slice(step * cut, (step + 1) * cut)
        both = jnp.concatenate([rows[:, columns], other_ref[:, columns]], axis=0)
        out_ref[:, columns] = jnp.dot(spots, both, preferred_element_type=jnp.float32).astype(
            jnp.bfloat16
        )


def place(base, own_ids, other_ids, own, other, chips):
    row_count, width = own.shape
    lines = chips * 2 * row_count // BLOCK_ROWS * BLOCK_SLOTS
    vmem = pl.BlockSpec(memory_space=pltpu.VMEM)
    return pl.pallas_call(
        functools.partial(place_kernel, chips),
        out_shape=pltpu.VMEM((lines, width), jnp.bfloat16),
        in_specs=[
            pl.BlockSpec(memory_space=pltpu.SMEM),
            vmem,
            vmem,
            pl.BlockSpec(memory_space=pl.ANY),
            vmem,
        ],
        out_specs=vmem,
        scratch_shapes=[
            pltpu.VMEM((row_count, width), jnp.bfloat16),
            pltpu.SemaphoreType.DMA((1,)),
        ],
        compiler_params=pltpu.CompilerParams(vmem_limit_bytes=12 << 20),
        name="place_rows",
    )(
        base,
        own_ids,
        other_ids,
        pltpu.with_memory_space_constraint(own, pltpu.HBM),
        pltpu.with_memory_space_constraint(other, pltpu.VMEM),
    )


def weigh_kernel(chips, base_ref, own_ids, other_ids, own_gates, other_gates, out_ref):
    columns = out_ref.shape[0] // 2
    matches, taken = expert_spots(own_ids[...], other_ids[...], base_ref[0], chips)
    gates = jnp.concatenate([own_gates[...], other_gates[...]], axis=1)
    route = gates / jnp.sum(gates, axis=0, keepdims=True)
    weight = sum(jnp.where(match, route[k : k + 1, :], 0.0) for k, match in enumerate(matches))
    weight = jnp.where(taken, weight, 0.0).T
    high = weight.astype(jnp.bfloat16)
    out_ref[:columns] = high
    out_ref[columns:] = (weight - high.astype(jnp.float32)).astype(jnp.bfloat16)


def weigh(base, own_ids, other_ids, own_gates, other_gates, lines):
    vmem = pl.BlockSpec(memory_space=pltpu.VMEM)
    chips = lines * BLOCK_ROWS // (2 * own_ids.shape[1] * BLOCK_SLOTS)
    return pl.pallas_call(
        functools.partial(weigh_kernel, chips),
        out_shape=jax.ShapeDtypeStruct((4 * own_ids.shape[1], lines), jnp.bfloat16),
        in_specs=[pl.BlockSpec(memory_space=pltpu.SMEM)] + [vmem] * 4,
        out_specs=vmem,
        compiler_params=pltpu.CompilerParams(vmem_limit_bytes=12 << 20),
        name="weigh_lines",
    )(base, own_ids, other_ids, own_gates, other_gates)


def mix_kernel(spread, in_hbm, own_ref, other_ref, lines, line_sems):
    row_count, width = own_ref.shape
    cut = width // MIX_PARTS

    def arrive(step):
        columns = pl.ds(step * cut, cut)
        return pltpu.make_async_copy(in_hbm.at[:, columns], lines.at[step], line_sems.at[step])

    for step in range(MIX_PARTS):
        arrive(step).start()
    for step in range(MIX_PARTS):
        arrive(step).wait()
        columns = slice(step * cut, (step + 1) * cut)
        total = jnp.dot(spread[...], lines[step], preferred_element_type=jnp.float32)
        total = total[: 2 * row_count] + total[2 * row_count :]
        own_ref[:, columns] = total[:row_count]
        other_ref[:, columns] = total[row_count:].astype(jnp.bfloat16)


def mix(spread, returned):
    row_count = spread.shape[0] // 4
    lines, width = returned.shape
    vmem = pl.BlockSpec(memory_space=pltpu.VMEM)
    return pl.pallas_call(
        mix_kernel,
        out_shape=(
            jax.ShapeDtypeStruct((row_count, width), jnp.float32),
            jax.ShapeDtypeStruct((row_count, width), jnp.bfloat16),
        ),
        in_specs=[vmem, pl.BlockSpec(memory_space=pl.ANY)],
        out_specs=(vmem, vmem),
        scratch_shapes=[
            pltpu.VMEM((MIX_PARTS, lines, width // MIX_PARTS), jnp.bfloat16),
            pltpu.SemaphoreType.DMA((MIX_PARTS,)),
        ],
        compiler_params=pltpu.CompilerParams(vmem_limit_bytes=12 << 20),
        name="mix_results",
    )(spread, pltpu.with_memory_space_constraint(returned, pltpu.HBM))


def expert_kernel(rows, in_ref, down_hbm, out_hbm, down, joint, hidden, out, down_sem, out_sems):
    row_count, width = rows.shape
    hidden_width = hidden.shape[1]
    block = row_count // ROW_PARTS
    cut = width // COLUMN_PARTS

    def leave(part, step):
        place = (pl.ds(part * block, block), pl.ds(step * cut, cut))
        return pltpu.make_async_copy(out.at[place], out_hbm.at[place], out_sems.at[part, step])

    fetch = pltpu.make_async_copy(down_hbm, down, down_sem.at[0])
    fetch.start()
    for part in range(ROW_PARTS):
        lines = slice(part * block, (part + 1) * block)
        joint[lines] = jnp.dot(rows[lines], in_ref[0], preferred_element_type=jnp.float32)
        gate = joint[lines, :hidden_width]
        hidden[lines] = (gate / (1.0 + jnp.exp(-gate)) * joint[lines, hidden_width:]).astype(
            jnp.bfloat16
        )
        if part == 0:
            fetch.wait()
        for step in range(COLUMN_PARTS):
            columns = slice(step * cut, (step + 1) * cut)
            out[lines, columns] = jnp.dot(
                hidden[lines], down[0, :, columns], preferred_element_type=jnp.float32
            ).astype(jnp.bfloat16)
            leave(part, step).start()
    for part in range(ROW_PARTS):
        for step in range(COLUMN_PARTS):
            leave(part, step).wait()


def expert(rows, expert_in, expert_down):
    row_count, width = rows.shape
    hidden_width = expert_down.shape[1]
    return pl.pallas_call(
        expert_kernel,
        out_shape=pltpu.HBM((row_count, width), jnp.bfloat16),
        in_specs=[
            pl.BlockSpec(memory_space=pltpu.VMEM),
            pl.BlockSpec(memory_space=pltpu.VMEM),
            pl.BlockSpec(memory_space=pl.ANY),
        ],
        out_specs=pl.BlockSpec(memory_space=pl.ANY),
        scratch_shapes=[
            pltpu.VMEM(expert_down.shape, jnp.bfloat16),
            pltpu.VMEM((row_count, 2 * hidden_width), jnp.float32),
            pltpu.VMEM((row_count, hidden_width), jnp.bfloat16),
            pltpu.VMEM((row_count, width), jnp.bfloat16),
            pltpu.SemaphoreType.DMA((1,)),
            pltpu.SemaphoreType.DMA((ROW_PARTS, COLUMN_PARTS)),
        ],
        compiler_params=pltpu.CompilerParams(vmem_limit_bytes=24 << 20),
        cost_estimate=pl.CostEstimate(
            flops=6 * row_count * width * hidden_width,
            bytes_accessed=4 * row_count * width,
            transcendentals=row_count * hidden_width,
        ),
        name="expert_layer",
    )(
        pltpu.with_memory_space_constraint(rows, pltpu.VMEM),
        pltpu.with_memory_space_constraint(expert_in, pltpu.VMEM),
        pltpu.with_memory_space_constraint(expert_down, pltpu.HBM),
    )


def body(
    queries,
    key_value_cache,
    guessed_key_value,
    cache_length_per_request,
    moe_rows,
    expert_ids,
    gate_weights,
    expert_in,
    expert_down,
):
    role = lax.axis_index("role")
    chips = lax.axis_size("dev")
    model_width = moe_rows.shape[1]
    swap = [(0, 1), (1, 0)]
    base = jnp.full((1,), role * chips, jnp.int32)

    def exchange(lines):
        blocks = lines.reshape(chips, -1, model_width)
        moved = lax.all_to_all(blocks, "dev", split_axis=0, concat_axis=0, tiled=True)
        return moved.reshape(-1, model_width)

    ids, gates = expert_ids.T, gate_weights.T
    other_ids = lax.ppermute(ids, "role", swap)
    other_rows = lax.ppermute(moe_rows, "role", swap)
    other_gates = lax.ppermute(gates, "role", swap)
    asked = (queries, key_value_cache, guessed_key_value, cache_length_per_request)
    attended = lax.cond(
        role == 1, attend_in_groups, lambda queries, *_: jnp.zeros_like(queries), *asked
    )
    other_rows, other_gates, attended = lax.optimization_barrier(
        (other_rows, other_gates, attended)
    )
    outgoing = place(base, ids, other_ids, moe_rows, other_rows, chips)
    outgoing, expert_in = lax.optimization_barrier((outgoing, expert_in))
    result = expert(exchange(outgoing), expert_in, expert_down)
    result, queries = lax.optimization_barrier((result, queries))
    returned = exchange(result)
    spread = weigh(base, ids, other_ids, gates, other_gates, result.shape[0])
    attended = lax.cond(
        role == 0,
        lambda done, *asked: attend_in_groups(*asked),
        lambda done, *_: done,
        attended,
        queries,
        *asked[1:],
    )
    returned, spread, attended = lax.optimization_barrier((returned, spread, attended))
    own, other = mix(spread, returned)
    received = lax.ppermute(other, "role", swap)
    mixed = (own + received.astype(jnp.float32)).astype(jnp.bfloat16)
    return (attended, mixed)


def solution(mesh):
    return jax.shard_map(
        body,
        mesh=mesh,
        in_specs=(
            P(("role", "dev"), None),
            P(("role", "dev"), None, None),
            P(("role", "dev"), None),
            P(("role", "dev")),
            P(("role", "dev"), None),
            P(("role", "dev"), None),
            P(("role", "dev"), None),
            P(("role", "dev"), None, None),
            P(("role", "dev"), None, None),
        ),
        out_specs=(P(("role", "dev"), None), P(("role", "dev"), None)),
        check_vma=False,
    )
```

```python
import functools

import jax
import jax.numpy as jnp
from jax import lax
from jax.experimental import pallas as pl
from jax.experimental.pallas import tpu as pltpu
from jax.sharding import PartitionSpec as P

QUERY_HEADS = 64
KEY_VALUE_HEADS = 4
HEAD_SIZE = 128
BLOCK_ROWS = 16
BLOCK_SLOTS = 2
ROW_PARTS = 2
COLUMN_PARTS = 4
MIX_PARTS = 4
ATTEND_CUTS = (2, 4)


def attend(queries, key_value_cache, guessed_key_value, cache_length_per_request):
    request_number, slot_positions, joint_width = key_value_cache.shape
    feature_width = joint_width // 2
    guessed_count = queries.shape[0] // request_number
    query_group_size = QUERY_HEADS // KEY_VALUE_HEADS
    scale = float(HEAD_SIZE) ** (-0.5)
    query_rows = queries.reshape(
        request_number, guessed_count, KEY_VALUE_HEADS, query_group_size, HEAD_SIZE
    )
    cache_key_rows = key_value_cache[:, :, :feature_width].reshape(
        request_number, slot_positions, KEY_VALUE_HEADS, HEAD_SIZE
    )
    cache_value_rows = key_value_cache[:, :, feature_width:].reshape(
        request_number, slot_positions, KEY_VALUE_HEADS, HEAD_SIZE
    )
    guessed_rows = guessed_key_value.reshape(request_number, guessed_count, joint_width)
    guessed_keys = guessed_rows[:, :, :feature_width].reshape(
        request_number, guessed_count, KEY_VALUE_HEADS, HEAD_SIZE
    )
    guessed_values = guessed_rows[:, :, feature_width:].reshape(
        request_number, guessed_count, KEY_VALUE_HEADS, HEAD_SIZE
    )
    scores_cache = (
        jnp.einsum(
            "rsngd,rcnd->rsngc", query_rows, cache_key_rows, preferred_element_type=jnp.float32
        )
        * scale
    )
    scores_fresh = (
        jnp.einsum(
            "rsngd,rjnd->rsngj", query_rows, guessed_keys, preferred_element_type=jnp.float32
        )
        * scale
    )
    valid_cache = (jnp.arange(slot_positions)[None, :] < cache_length_per_request[:, None])[
        :, None, None, None, :
    ]
    valid_fresh = (jnp.arange(guessed_count)[None, :] <= jnp.arange(guessed_count)[:, None])[
        None, :, None, None, :
    ]
    scores_cache = jnp.where(valid_cache, scores_cache, -jnp.inf)
    scores_fresh = jnp.where(valid_fresh, scores_fresh, -jnp.inf)
    highest = jnp.maximum(
        jnp.max(scores_cache, axis=-1, keepdims=True), jnp.max(scores_fresh, axis=-1, keepdims=True)
    )
    exp_cache = jnp.exp(scores_cache - highest)
    exp_fresh = jnp.exp(scores_fresh - highest)
    total = jnp.sum(exp_cache, axis=-1, keepdims=True) + jnp.sum(exp_fresh, axis=-1, keepdims=True)
    probs_cache = (exp_cache / total).astype(jnp.bfloat16)
    probs_fresh = (exp_fresh / total).astype(jnp.bfloat16)
    output = jnp.einsum(
        "rsngc,rcnd->rsngd", probs_cache, cache_value_rows, preferred_element_type=jnp.float32
    )
    output = output + jnp.einsum(
        "rsngj,rjnd->rsngd", probs_fresh, guessed_values, preferred_element_type=jnp.float32
    )
    return output.reshape(request_number * guessed_count, QUERY_HEADS * HEAD_SIZE).astype(
        jnp.bfloat16
    )


def attend_in_groups(queries, key_value_cache, guessed_key_value, cache_length_per_request):
    arrays = (queries, key_value_cache, guessed_key_value, cache_length_per_request)
    requests = key_value_cache.shape[0]
    groups = zip(
        *(
            jnp.split(array, [cut * array.shape[0] // requests for cut in ATTEND_CUTS])
            for array in arrays
        )
    )
    done = []
    for group in groups:
        if done:
            done[-1], group = lax.optimization_barrier((done[-1], group))
        done.append(attend(*group))
    return jnp.concatenate(done)


def expert_spots(own_ids, other_ids, base, chips):
    ids = jnp.concatenate([own_ids, other_ids], axis=1)
    top_count, columns = ids.shape
    slots = columns // BLOCK_ROWS * BLOCK_SLOTS
    shape = (chips * slots, columns)
    line = lax.broadcasted_iota(jnp.int32, shape, 0)
    column = lax.broadcasted_iota(jnp.int32, shape, 1)
    serving = base + line // slots
    matches = [ids[k : k + 1, :] == serving for k in range(top_count)]
    member = functools.reduce(jnp.logical_or, matches)
    here = lax.broadcasted_iota(jnp.int32, (columns, columns), 0)
    there = lax.broadcasted_iota(jnp.int32, (columns, columns), 1)
    earlier = (here < there) & (here // BLOCK_ROWS == there // BLOCK_ROWS)
    ranks = jnp.dot(
        jnp.where(member, 1.0, 0.0).astype(jnp.bfloat16),
        jnp.where(earlier, 1.0, 0.0).astype(jnp.bfloat16),
        preferred_element_type=jnp.float32,
    ).astype(jnp.int32)
    return matches, member & (column // BLOCK_ROWS * BLOCK_SLOTS + ranks == line % slots)


def spots_kernel(chips, base_ref, own_ids, other_ids, out_ref):
    _, taken = expert_spots(own_ids[...], other_ids[...], base_ref[0], chips)
    out_ref[...] = jnp.where(taken, 1.0, 0.0).astype(jnp.bfloat16)


def find_spots(base, own_ids, other_ids, chips):
    columns = 2 * own_ids.shape[1]
    lines = chips * columns // BLOCK_ROWS * BLOCK_SLOTS
    vmem = pl.BlockSpec(memory_space=pltpu.VMEM)
    return pl.pallas_call(
        functools.partial(spots_kernel, chips),
        out_shape=pltpu.VMEM((lines, columns), jnp.bfloat16),
        in_specs=[pl.BlockSpec(memory_space=pltpu.SMEM), vmem, vmem],
        out_specs=vmem,
        compiler_params=pltpu.CompilerParams(vmem_limit_bytes=8 << 20),
        name="find_spots",
    )(base, own_ids, other_ids)


def place_kernel(spots, own_hbm, other_ref, out_ref, rows, row_sem):
    fetch = pltpu.make_async_copy(own_hbm, rows, row_sem.at[0])
    fetch.start()
    fetch.wait()
    cut = rows.shape[1] // COLUMN_PARTS
    for step in range(COLUMN_PARTS):
        columns = slice(step * cut, (step + 1) * cut)
        both = jnp.concatenate([rows[:, columns], other_ref[:, columns]], axis=0)
        out_ref[:, columns] = jnp.dot(
            spots[...], both, preferred_element_type=jnp.float32
        ).astype(jnp.bfloat16)


def place(spots, own, other):
    row_count, width = own.shape
    vmem = pl.BlockSpec(memory_space=pltpu.VMEM)
    return pl.pallas_call(
        place_kernel,
        out_shape=pltpu.VMEM((spots.shape[0], width), jnp.bfloat16),
        in_specs=[vmem, pl.BlockSpec(memory_space=pl.ANY), vmem],
        out_specs=vmem,
        scratch_shapes=[
            pltpu.VMEM((row_count, width), jnp.bfloat16),
            pltpu.SemaphoreType.DMA((1,)),
        ],
        compiler_params=pltpu.CompilerParams(vmem_limit_bytes=12 << 20),
        name="place_rows",
    )(
        spots,
        pltpu.with_memory_space_constraint(own, pltpu.HBM),
        pltpu.with_memory_space_constraint(other, pltpu.VMEM),
    )


def weigh_kernel(chips, base_ref, own_ids, other_ids, own_gates, other_gates, out_ref):
    columns = out_ref.shape[0] // 2
    matches, taken = expert_spots(own_ids[...], other_ids[...], base_ref[0], chips)
    gates = jnp.concatenate([own_gates[...], other_gates[...]], axis=1)
    route = gates / jnp.sum(gates, axis=0, keepdims=True)
    weight = sum(jnp.where(match, route[k : k + 1, :], 0.0) for k, match in enumerate(matches))
    weight = jnp.where(taken, weight, 0.0).T
    high = weight.astype(jnp.bfloat16)
    out_ref[:columns] = high
    out_ref[columns:] = (weight - high.astype(jnp.float32)).astype(jnp.bfloat16)


def weigh(base, own_ids, other_ids, own_gates, other_gates, lines):
    vmem = pl.BlockSpec(memory_space=pltpu.VMEM)
    chips = lines * BLOCK_ROWS // (2 * own_ids.shape[1] * BLOCK_SLOTS)
    return pl.pallas_call(
        functools.partial(weigh_kernel, chips),
        out_shape=jax.ShapeDtypeStruct((4 * own_ids.shape[1], lines), jnp.bfloat16),
        in_specs=[pl.BlockSpec(memory_space=pltpu.SMEM)] + [vmem] * 4,
        out_specs=vmem,
        compiler_params=pltpu.CompilerParams(vmem_limit_bytes=12 << 20),
        name="weigh_lines",
    )(base, own_ids, other_ids, own_gates, other_gates)


def mix_kernel(spread, in_hbm, own_ref, other_ref, lines, line_sems):
    row_count, width = own_ref.shape
    cut = width // MIX_PARTS

    def arrive(step):
        columns = pl.ds(step * cut, cut)
        return pltpu.make_async_copy(in_hbm.at[:, columns], lines.at[step], line_sems.at[step])

    for step in range(MIX_PARTS):
        arrive(step).start()
    for step in range(MIX_PARTS):
        arrive(step).wait()
        columns = slice(step * cut, (step + 1) * cut)
        total = jnp.dot(spread[...], lines[step], preferred_element_type=jnp.float32)
        total = total[: 2 * row_count] + total[2 * row_count :]
        own_ref[:, columns] = total[:row_count]
        other_ref[:, columns] = total[row_count:].astype(jnp.bfloat16)


def mix(spread, returned):
    row_count = spread.shape[0] // 4
    lines, width = returned.shape
    vmem = pl.BlockSpec(memory_space=pltpu.VMEM)
    return pl.pallas_call(
        mix_kernel,
        out_shape=(
            jax.ShapeDtypeStruct((row_count, width), jnp.float32),
            jax.ShapeDtypeStruct((row_count, width), jnp.bfloat16),
        ),
        in_specs=[vmem, pl.BlockSpec(memory_space=pl.ANY)],
        out_specs=(vmem, vmem),
        scratch_shapes=[
            pltpu.VMEM((MIX_PARTS, lines, width // MIX_PARTS), jnp.bfloat16),
            pltpu.SemaphoreType.DMA((MIX_PARTS,)),
        ],
        compiler_params=pltpu.CompilerParams(vmem_limit_bytes=12 << 20),
        name="mix_results",
    )(spread, pltpu.with_memory_space_constraint(returned, pltpu.HBM))


def expert_kernel(rows, in_ref, down_hbm, out_hbm, down, joint, hidden, out, down_sem, out_sems):
    row_count, width = rows.shape
    hidden_width = hidden.shape[1]
    block = row_count // ROW_PARTS
    cut = width // COLUMN_PARTS

    def leave(part, step):
        place = (pl.ds(part * block, block), pl.ds(step * cut, cut))
        return pltpu.make_async_copy(out.at[place], out_hbm.at[place], out_sems.at[part, step])

    fetch = pltpu.make_async_copy(down_hbm, down, down_sem.at[0])
    fetch.start()
    for part in range(ROW_PARTS):
        lines = slice(part * block, (part + 1) * block)
        joint[lines] = jnp.dot(rows[lines], in_ref[0], preferred_element_type=jnp.float32)
        gate = joint[lines, :hidden_width]
        hidden[lines] = (gate / (1.0 + jnp.exp(-gate)) * joint[lines, hidden_width:]).astype(
            jnp.bfloat16
        )
        if part == 0:
            fetch.wait()
        for step in range(COLUMN_PARTS):
            columns = slice(step * cut, (step + 1) * cut)
            out[lines, columns] = jnp.dot(
                hidden[lines], down[0, :, columns], preferred_element_type=jnp.float32
            ).astype(jnp.bfloat16)
            leave(part, step).start()
    for part in range(ROW_PARTS):
        for step in range(COLUMN_PARTS):
            leave(part, step).wait()


def expert(rows, expert_in, expert_down):
    row_count, width = rows.shape
    hidden_width = expert_down.shape[1]
    return pl.pallas_call(
        expert_kernel,
        out_shape=pltpu.HBM((row_count, width), jnp.bfloat16),
        in_specs=[
            pl.BlockSpec(memory_space=pltpu.VMEM),
            pl.BlockSpec(memory_space=pltpu.VMEM),
            pl.BlockSpec(memory_space=pl.ANY),
        ],
        out_specs=pl.BlockSpec(memory_space=pl.ANY),
        scratch_shapes=[
            pltpu.VMEM(expert_down.shape, jnp.bfloat16),
            pltpu.VMEM((row_count, 2 * hidden_width), jnp.float32),
            pltpu.VMEM((row_count, hidden_width), jnp.bfloat16),
            pltpu.VMEM((row_count, width), jnp.bfloat16),
            pltpu.SemaphoreType.DMA((1,)),
            pltpu.SemaphoreType.DMA((ROW_PARTS, COLUMN_PARTS)),
        ],
        compiler_params=pltpu.CompilerParams(vmem_limit_bytes=24 << 20),
        cost_estimate=pl.CostEstimate(
            flops=6 * row_count * width * hidden_width,
            bytes_accessed=4 * row_count * width,
            transcendentals=row_count * hidden_width,
        ),
        name="expert_layer",
    )(
        pltpu.with_memory_space_constraint(rows, pltpu.VMEM),
        pltpu.with_memory_space_constraint(expert_in, pltpu.VMEM),
        pltpu.with_memory_space_constraint(expert_down, pltpu.HBM),
    )


def body(
    queries,
    key_value_cache,
    guessed_key_value,
    cache_length_per_request,
    moe_rows,
    expert_ids,
    gate_weights,
    expert_in,
    expert_down,
):
    role = lax.axis_index("role")
    chips = lax.axis_size("dev")
    model_width = moe_rows.shape[1]
    swap = [(0, 1), (1, 0)]
    base = jnp.full((1,), role * chips, jnp.int32)

    def exchange(lines):
        blocks = lines.reshape(chips, -1, model_width)
        moved = lax.all_to_all(blocks, "dev", split_axis=0, concat_axis=0, tiled=True)
        return moved.reshape(-1, model_width)

    ids, gates = expert_ids.T, gate_weights.T
    other_ids = lax.ppermute(ids, "role", swap)
    other_rows = lax.ppermute(moe_rows, "role", swap)
    other_gates = lax.ppermute(gates, "role", swap)
    asked = (queries, key_value_cache, guessed_key_value, cache_length_per_request)
    attended = lax.cond(
        role == 1, attend_in_groups, lambda queries, *_: jnp.zeros_like(queries), *asked
    )
    spots = find_spots(base, ids, other_ids, chips)
    spots, other_rows, other_gates, attended = lax.optimization_barrier(
        (spots, other_rows, other_gates, attended)
    )
    outgoing = place(spots, moe_rows, other_rows)
    outgoing, expert_in = lax.optimization_barrier((outgoing, expert_in))
    result = expert(exchange(outgoing), expert_in, expert_down)
    result, queries = lax.optimization_barrier((result, queries))
    returned = exchange(result)
    spread = weigh(base, ids, other_ids, gates, other_gates, result.shape[0])
    attended = lax.cond(
        role == 0,
        lambda done, *asked: attend_in_groups(*asked),
        lambda done, *_: done,
        attended,
        queries,
        *asked[1:],
    )
    returned, spread, attended = lax.optimization_barrier((returned, spread, attended))
    own, other = mix(spread, returned)
    received = lax.ppermute(other, "role", swap)
    mixed = (own + received.astype(jnp.float32)).astype(jnp.bfloat16)
    return (attended, mixed)


def solution(mesh):
    return jax.shard_map(
        body,
        mesh=mesh,
        in_specs=(
            P(("role", "dev"), None),
            P(("role", "dev"), None, None),
            P(("role", "dev"), None),
            P(("role", "dev")),
            P(("role", "dev"), None),
            P(("role", "dev"), None),
            P(("role", "dev"), None),
            P(("role", "dev"), None, None),
            P(("role", "dev"), None, None),
        ),
        out_specs=(P(("role", "dev"), None), P(("role", "dev"), None)),
        check_vma=False,
    )
```
